256 devices in a mesh: seg: 8 (over y, core), sec: 32 (over z, x).
Axes of the slice: x: 4, y: 4, z: 8, core: 2. Of those that a mesh axis runs over, the one named last changes fastest.
Arguments:
- state_blocks: bfloat16 [8, 64, 256, 256], P('seg', 'sec')
- gauge_offset: float32 [8, 64, 256, 256], P('seg', 'sec'), may hold values from -0.1125 to 0.1125
- left_env: bfloat16 [8, 64, 16, 256, 256], P('seg', 'sec'), may hold values from -0.09375 to 0.09375
- right_env: bfloat16 [8, 64, 16, 256, 256], P('seg', 'sec'), may hold values from -0.375 to 0.375
- mpo_mask: int32 [64, 16], P('sec'), may hold values 0 or 1
- charge: int32 [16], replicated, may hold values from -1 to 1, as said below
- block_dims: int32 [64], P('sec'), may hold values from 64 to 256, as said below
Outputs:
- krylov: bfloat16 [8, 64, 256, 256], P('seg', 'sec')
- env_next: bfloat16 [8, 64, 16, 256, 256], P('seg', 'sec')
- rayleigh: float32 [8], P('seg')
The draws below stay inside these ranges and needn't reach their ends.
Inputs may be any that keep to these rules, and one draw needn't show every extreme that they name: `charge`: exactly 4 channels carry +1 and exactly 4 carry -1, the others 0. `block_dims`: some sector has exactly 256 live rows in every draw.
All inputs are finite; a program needn't handle non-finite values. No bound on the sum of `mpo_mask` on one device may be relied on, other than what follows from the above.
Results may differ from the reference program's by a relative error of at most 0.018.
Values may be sent and summed in bfloat16 or wider, within the bound.
No kernel may reach another device: no remote copies, remote signals or barrier semaphores. Data moves between devices by JAX's collectives and lax.ppermute only.
A program may use at most 64 MiB of HBM per device.

```python
import jax
import jax.numpy as jnp
from jax import lax

B = 256
W = 16
SECTORS = 64
SEGMENTS = 8


def draw_state_blocks(key, part):
    key = jax.random.fold_in(key, 11)
    position = jnp.arange(SECTORS, dtype=jnp.float32) / max(SECTORS - 1, 1)
    values_drawn = jax.random.normal(key, (SEGMENTS, SECTORS, B, B), jnp.float32)
    sector_scale = 3.0 ** position
    return (values_drawn * sector_scale[None, :, None, None]).astype(jnp.bfloat16)


def draw_charge(key, part):
    key = jax.random.fold_in(key, 23)
    shuffled = jax.random.permutation(key, W)
    quarter = W // 4
    return jnp.where(shuffled < quarter, 1, jnp.where(shuffled >= W - quarter, -1, 0)).astype(jnp.int32)


def draw_block_dims(key, part):
    key = jax.random.fold_in(key, 37)
    first_key, second_key = jax.random.split(key)
    drawn_dims = jax.random.randint(first_key, (SECTORS,), B // 4, B + 1).astype(jnp.int32)
    full_sector = jax.random.randint(second_key, (), 0, SECTORS)
    return drawn_dims.at[full_sector].set(B).astype(jnp.int32)


def set_ends(entries, key, low, largest):
    extent = entries.shape
    place = [jax.random.randint(jax.random.fold_in(key, axis), (), 0, extent[axis]) for axis in range(len(extent))]
    entries = entries.at[tuple(place)].set(low)
    longest = extent.index(max(extent))
    place[longest] = (place[longest] + 1) % extent[longest]
    return entries.at[tuple(place)].set(largest)


def levels(key, dims, shards, least, largest):
    level, own = 1.0, jax.random.fold_in(key, 6)
    for dim, shards_of in shards:
        draws = jnp.exp(jax.random.uniform(jax.random.fold_in(own, dim), (shards_of,), jnp.float32, least / len(shards), largest / len(shards)))
        level = level * jnp.repeat(draws, dims[dim] // shards_of).reshape([-1 if axis == dim else 1 for axis in range(len(dims))])
    return level


def gaussian(key, shape, spread, reach, cuts=(), kind=jnp.bfloat16):
    entries = spread * jax.random.normal(key, shape, jnp.float32)
    if cuts:
        entries = entries * levels(key, shape, cuts, -0.22, 0.18)
    return jnp.clip(entries, -reach, reach).astype(kind)


def setup_inputs(seed: int = 0) -> dict:
    seeds = jax.random.split(jax.random.key(seed), 8)
    return {
        "state_blocks": draw_state_blocks(jax.random.fold_in(seeds[7], 71), 0),
        "gauge_offset": gaussian(seeds[1], (SEGMENTS, SECTORS, B, B), (0.3 * B ** -0.5), 0.1125, ((0, 8), (1, 32)), jnp.float32),
        "left_env": gaussian(seeds[2], (SEGMENTS, SECTORS, W, B, B), (B * W) ** -0.5, 0.09375, ((0, 8), (1, 32))),
        "right_env": gaussian(seeds[3], (SEGMENTS, SECTORS, W, B, B), B ** -0.5, 0.375, ((0, 8), (1, 32))),
        "mpo_mask": set_ends((jax.random.randint(seeds[4], (SECTORS, W), 0, 4) < 3).astype(jnp.int32), jax.random.fold_in(seeds[4], 1), 0, 1),
        "charge": draw_charge(jax.random.fold_in(seeds[7], 71), 0),
        "block_dims": draw_block_dims(jax.random.fold_in(seeds[7], 71), 0),
    }


def cell_of(block_dims):
    live_rows = jnp.arange(B)[None, :] < block_dims[:, None]
    return (live_rows[:, :, None] & live_rows[:, None, :]).astype(jnp.float32)

def shifted(field, charge):
    zero_block = jnp.zeros((1,) + field.shape[1:], field.dtype)
    padded = jnp.concatenate([zero_block, field, zero_block], 0)
    below = padded[:-2]
    above = padded[2:]
    if field.ndim == 3:
        below = below[:, None]
        above = above[:, None]
        middle = field[:, None]
    else:
        middle = field
    upward = (charge == 1)[None, :, None, None]
    downward = (charge == -1)[None, :, None, None]
    return jnp.where(upward, below, jnp.where(downward, above, middle))

def hamiltonian(field, left_env, right_env, mpo_mask, charge, cell_mask):
    select = shifted(field, charge)
    partial_value = jnp.einsum('gwij,gwjk->gwik', left_env.astype(jnp.float32), select.astype(jnp.float32)).astype(jnp.bfloat16)
    partial_value = partial_value.astype(jnp.float32) * mpo_mask[:, :, None, None].astype(jnp.float32)
    image = jnp.einsum('gwij,gwjk->gik', partial_value, right_env.astype(jnp.float32))
    return (image * cell_mask).astype(jnp.bfloat16)

def reference(state_blocks, gauge_offset, left_env, right_env, mpo_mask, charge, block_dims):
    identity_blocks = jnp.broadcast_to(jnp.eye(B, dtype=jnp.float32), (SECTORS, B, B))
    gauge = gauge_offset + identity_blocks[None]

    def advance(carry, factor):
        product = jnp.einsum('gij,gjk->gik', factor, carry, precision=lax.Precision.HIGHEST)
        return (product, product)
    unused, prefix = lax.scan(advance, identity_blocks, gauge)
    cell_mask = cell_of(block_dims)

    def segment(items):
        prefix_here, state_here, left_here, right_here = items
        x = (jnp.einsum('gij,gjk->gik', prefix_here, state_here.astype(jnp.float32), precision=lax.Precision.HIGHEST) * cell_mask).astype(jnp.bfloat16)
        first = hamiltonian(x, left_here, right_here, mpo_mask, charge, cell_mask)
        x_wide = x.astype(jnp.float32)
        first_wide = first.astype(jnp.float32)
        norm_state = jnp.sum(x_wide * x_wide)
        correlation = jnp.sum(x_wide * first_wide)
        rayleigh = correlation / norm_state
        residue = first_wide - rayleigh * x_wide
        residue_scale = jnp.sqrt(jnp.sum(residue * residue) / (SECTORS * B * B) + 1e-06)
        lanczos_vec = (residue / residue_scale).astype(jnp.bfloat16)
        krylov = hamiltonian(lanczos_vec, left_here, right_here, mpo_mask, charge, cell_mask)
        left_x = jnp.einsum('gwij,gjk->gwik', left_here.astype(jnp.float32), x_wide).astype(jnp.bfloat16)
        contrib = jnp.einsum('gia,gwij->gwaj', x_wide, left_x.astype(jnp.float32)).astype(jnp.bfloat16)
        env_next = shifted(contrib, charge)
        return (krylov, env_next, rayleigh)
    krylov, env_next, rayleigh = lax.map(segment, (prefix, state_blocks, left_env, right_env))
    return (krylov, env_next, rayleigh)
```

```python
import functools

import jax
import jax.numpy as jnp
from jax import lax
from jax.experimental import pallas as pl
from jax.experimental.pallas import tpu as pltpu
from jax.sharding import PartitionSpec as P

F32 = jnp.float32
BF16 = jnp.bfloat16
AXES = ("seg", "sec")
QUARTER = 4
MIB = 1 << 20


def dot(first, second):
    return lax.dot_general(
        first, second, (((1,), (0,)), ((), ())), preferred_element_type=F32
    )


def vmem(count):
    return [pl.BlockSpec(memory_space=pltpu.VMEM)] * count


def smem(count):
    return [pl.BlockSpec(memory_space=pltpu.SMEM)] * count


def anywhere(count):
    return [pl.BlockSpec(memory_space=pl.ANY)] * count


def cost(products, size, bytes_accessed):
    return pl.CostEstimate(
        flops=2 * products * size**3, bytes_accessed=bytes_accessed, transcendentals=0
    )


def place():
    position = lax.axis_index("seg")
    return position % 2, position // 2


def limit(mebibytes):
    return pltpu.CompilerParams(vmem_limit_bytes=mebibytes * MIB)


def live(dim, size):
    rows = lax.broadcasted_iota(jnp.int32, (size, size), 0) < dim
    columns = lax.broadcasted_iota(jnp.int32, (size, size), 1) < dim
    return rows & columns


def in_hbm(array):
    return pltpu.with_memory_space_constraint(array, pltpu.HBM)


def split_kernel(gauge, state, own, other, gauge_here, state_here, sems):
    core = place()[0]
    arrivals = [
        pltpu.make_async_copy(gauge, gauge_here, sems.at[0]),
        pltpu.make_async_copy(state, state_here, sems.at[1]),
    ]
    for copy in arrivals:
        copy.start()
    for copy in arrivals:
        copy.wait()
    own[0] = gauge_here[core].astype(BF16)
    own[1] = state_here[core]
    other[0] = gauge_here[1 - core].astype(BF16)
    other[1] = state_here[1 - core]


def table_kernel(charge_far, mask_far, dims_far, left, cells, to_left, to_right, table, charge,
                 mask, dims, sems, cross_sems):
    channels, size = left.shape[1], left.shape[2]
    arrivals = [
        pltpu.make_async_copy(charge_far, charge, sems.at[0]),
        pltpu.make_async_copy(mask_far, mask, sems.at[1]),
        pltpu.make_async_copy(dims_far, dims, sems.at[2]),
    ]
    for copy in arrivals:
        copy.start()
    for copy in arrivals:
        copy.wait()
    ups, downs, rest = jnp.int32(0), jnp.int32(0), jnp.int32(0)
    for w in range(channels):
        up, down = charge[w] == 1, charge[w] == -1
        middle = QUARTER + rest
        table[0, jnp.where(up, ups, jnp.where(down, channels - QUARTER + downs, middle))] = w
        table[1, jnp.where(down, downs, jnp.where(up, channels - QUARTER + ups, middle))] = w
        ups = ups + up.astype(jnp.int32)
        downs = downs + down.astype(jnp.int32)
        rest = rest + jnp.where(up | down, 0, 1)
    crossings = []
    for s in range(2):
        for j in range(QUARTER):
            w = table[s, channels - QUARTER + j]
            crossings.append(
                pltpu.make_async_copy(
                    left.at[s, w], (to_left, to_right)[s].at[j], cross_sems.at[s, j]
                )
            )
            crossings[-1].start()
    for s in range(2):
        for j in range(channels):
            table[2 + s, j] = mask[s, table[s, j]]
        cells[s] = jnp.where(live(dims[s], size), 1.0, 0.0).astype(BF16)
    for copy in crossings:
        copy.wait()


def sort_kernel(masked, table, source, target, sems):
    channels = source.shape[1]

    def copy(s, j):
        return pltpu.make_async_copy(
            source.at[s, table[s, j]], target.at[s, j], sems.at[s, j]
        )

    for s in range(2):
        for j in range(channels):
            copy(s, j).start()
    for s in range(2):
        for j in range(channels):
            copy(s, j).wait()
            if masked:
                @pl.when(table[2 + s, j] == 0)
                def _():
                    target[s, j] = jnp.zeros(target.shape[2:], target.dtype)


def joined(later, earlier):
    return later.astype(F32) + earlier.astype(F32) + dot(later, earlier)


def pair_kernel(own, got, after, out):
    core = place()[0]

    @pl.when(core == 0)
    def _():
        out[...] = joined(got[0], own[0]).astype(BF16)

    @pl.when(core == 1)
    def _():
        out[...] = joined(own[0], got[0]).astype(BF16)


def four_kernel(own, got, after, out):
    chip = place()[1]

    @pl.when(chip % 2 == 0)
    def _():
        out[...] = joined(got[...], own[...]).astype(BF16)

    @pl.when(chip % 2 == 1)
    def _():
        out[...] = joined(own[...], got[...]).astype(BF16)


def state_kernel(cells, own, got, near, far, *refs):
    x_own, x_other, pair = refs[-3:]
    core, chip = place()
    size = x_own.shape[0]
    pair[core] = own[...]
    pair[1 - core] = got[...]
    field = jnp.concatenate([pair[0, 1], pair[1, 1]], axis=1)
    wide = field.astype(F32)
    wide = wide + dot(far[...], field)
    near_here = jnp.where(chip != 0, near[...].astype(F32), 0.0).astype(BF16)
    wide = wide + dot(near_here, wide.astype(BF16))
    wide = wide + dot(pair[0, 0], wide.astype(BF16))
    earlier, later = wide[:, :size], wide[:, size:]
    later = later + dot(pair[1, 0], later.astype(BF16))
    alive = cells[core] != 0
    first = jnp.where(alive, earlier, 0.0).astype(BF16)
    second = jnp.where(alive, later, 0.0).astype(BF16)
    x_own[...] = jnp.where(core == 0, first, second)
    x_other[...] = jnp.where(core == 0, second, first)


def spread(parts, s, blocks, field, first, last):
    size = field.shape[0]
    rows = blocks[s, first:last].reshape((last - first) * size, size)
    result = dot(rows, field).astype(BF16)
    for j in range(first, last):
        at = (j - first) * size
        parts[s, :, j * size : (j + 1) * size] = result[at : at + size]


def folded(parts, s, blocks, first, last):
    size = blocks.shape[-1]
    rows = blocks[s, first:last].reshape((last - first) * size, size)
    return dot(parts[s, :, first * size : last * size], rows)


def own_kernel(x_own, x_got, left, right, table_far, acc, env, x_here, parts, blocks, table,
               table_sem, out_sems):
    core = place()[0]
    channels, size = left.shape[1], left.shape[2]
    cross = channels - QUARTER
    fetch = pltpu.make_async_copy(table_far, table, table_sem.at[0])
    fetch.start()
    x_here[core] = x_own[...]
    x_here[1 - core] = x_got[...]

    def send(s, j):
        target = 1 - s if j < QUARTER else s
        return pltpu.make_async_copy(
            blocks.at[s, j], env.at[0, target, table[s, j]], out_sems.at[s, j]
        )

    for s in range(2):
        field = x_here[s]
        turned = field.T
        spread(parts, s, left, field, 0, cross)
        result = dot(turned, parts[s, :, : cross * size]).astype(BF16)
        for j in range(cross):
            blocks[s, j] = result[:, j * size : (j + 1) * size]
        if s == 0:
            fetch.wait()
        for j in range(cross):
            send(s, j).start()
    for s in range(2):
        spread(parts, s, left, x_here[1 - s], cross, channels)
        acc[s] = folded(parts, s, right, QUARTER, channels)
    for s in range(2):
        for j in range(cross):
            send(s, j).wait()


def image_kernel(cells, x_here, side_same, side_cross, left_side, right_side, acc, v_first,
                 v_second, sums, x_side, parts):
    core = place()[0]
    x_side[1 - core] = side_same[...]
    x_side[core] = side_cross[...]
    total = []
    for s in range(2):
        spread(parts, s, left_side, x_side[s], 0, QUARTER)
        image = acc[s] + folded(parts, s, right_side, 0, QUARTER)
        image = jnp.where(cells[s] != 0, image, 0.0).astype(BF16)
        (v_first, v_second)[s][...] = image
        total.append(image)

    def whole(values):
        return jnp.sum(jnp.sum(values, axis=0, keepdims=True), axis=1, keepdims=True)

    x_wide = [x_here[s].astype(F32) for s in range(2)]
    v_wide = [total[s].astype(F32) for s in range(2)]
    norm = whole(x_wide[0] * x_wide[0] + x_wide[1] * x_wide[1])
    correlation = whole(x_wide[0] * v_wide[0] + x_wide[1] * v_wide[1])
    ratio = jnp.where(norm > 0.0, correlation / jnp.where(norm > 0.0, norm, 1.0), 0.0)
    apart = [v_wide[s] - ratio * x_wide[s] for s in range(2)]
    spread_of = whole(apart[0] * apart[0] + apart[1] * apart[1])
    lane = lax.broadcasted_iota(jnp.int32, sums.shape, 1)
    row = jnp.where(lane == 0, norm, jnp.where(lane == 1, correlation, 0.0))
    row = jnp.where(lane == 2, ratio, jnp.where(lane == 3, spread_of, row))
    sums[...] = row


def krylov_kernel(total_cells, cells, sums, x_here, x_side, v_first, v_second, v_left, v_right,
                  left_up, left_down, table_far, charge_far, mask_far, left, right, env_in,
                  krylov, env, rayleigh, left_here, right_here, fields, parts, side_parts,
                  blocks, table, charge, mask, sems, small_sems, out_sems):
    channels, size = left.shape[1], left.shape[2]
    half = channels // 2
    steps = [(side, s, h) for s in range(2) for side in range(2) for h in range(2)]

    def load(step):
        side, s, h = steps[step]
        source, target = ((left, left_here), (right, right_here))[side]
        span = pl.ds(h * half, half)
        return pltpu.make_async_copy(source.at[s, span], target.at[s, span], sems.at[step])

    small = [
        pltpu.make_async_copy(table_far, table, small_sems.at[0]),
        pltpu.make_async_copy(charge_far, charge, small_sems.at[1]),
        pltpu.make_async_copy(mask_far, mask, small_sems.at[2]),
    ]
    for copy in small:
        copy.start()
    ahead = 3
    for step in range(ahead):
        load(step).start()

    column = [jnp.sum(sums[:, i : i + 1], axis=0, keepdims=True) for i in range(2)]
    ratio = column[1] / column[0]
    apart = ratio - sums[:, 2:3]
    spread_of = jnp.sum(sums[:, 3:4] + apart * apart * sums[:, 0:1], axis=0, keepdims=True)
    inverse = 1.0 / jnp.sqrt(spread_of * (1.0 / total_cells) + 1e-06)
    rayleigh[0] = ratio[0, 0]

    def scaled(v, x):
        return ((v.astype(F32) - ratio * x.astype(F32)) * inverse).astype(BF16)

    fields[0] = scaled(v_left[...], x_side[0])
    fields[1] = scaled(v_first[...], x_here[0])
    fields[2] = scaled(v_second[...], x_here[1])
    fields[3] = scaled(v_right[...], x_side[1])

    def send(s, j):
        return pltpu.make_async_copy(
            blocks.at[s, j], env.at[0, s, table[s, j]], out_sems.at[s, j]
        )

    for s in range(2):
        turned = x_side[s].T
        arriving = (left_up, left_down)[s]
        lx = dot(arriving[...].reshape(QUARTER * size, size), x_side[s]).astype(BF16)
        for j in range(QUARTER):
            side_parts[:, j * size : (j + 1) * size] = lx[j * size : (j + 1) * size]
        result = dot(turned, side_parts[...]).astype(BF16)
        for j in range(QUARTER):
            blocks[s, j] = result[:, j * size : (j + 1) * size]
    for copy in small:
        copy.wait()
    for s in range(2):
        for j in range(QUARTER):
            send(s, j).start()

    image = None
    for step, (side, s, h) in enumerate(steps):
        load(step).wait()
        if step + ahead < len(steps):
            load(step + ahead).start()
        span = range(h * half, (h + 1) * half)
        if side == 0:
            for w in span:
                part = dot(left_here[s, w], fields[s + 1 - charge[w]])
                part = part * mask[s, w].astype(F32)
                parts[:, w * size : (w + 1) * size] = part.astype(BF16)
        else:
            rows = right_here[s, h * half : (h + 1) * half].reshape(half * size, size)
            product = dot(parts[:, h * half * size : (h + 1) * half * size], rows)
            image = product if h == 0 else image + product
            if h == 1:
                krylov[0, s] = jnp.where(cells[s] != 0, image, 0.0).astype(BF16)
    for s in range(2):
        for j in range(QUARTER):
            send(s, j).wait()


def local(state_blocks, gauge_offset, left_env, right_env, mpo_mask, charge, block_dims):
    size = state_blocks.shape[-1]
    channels = left_env.shape[2]
    segments = lax.axis_size("seg")
    groups = lax.axis_size("sec")
    block = (size, size)

    def at(segment, group):
        return segment * groups + group

    every = range(groups)
    swap = [(at(k, i), at(k ^ 1, i)) for k in range(segments) for i in every]
    chip_pairs = [
        (at(2 * a + r, i), at(2 * b + r, i))
        for a, b in ((0, 1), (1, 0), (2, 3)) for r in range(2) for i in every
    ]
    far_pairs = [
        (at(2 * a + r, i), at(2 * b + r, i))
        for a, b in ((1, 2), (0, 3)) for r in range(2) for i in every
    ]
    same, cross = [], []
    for c in range(segments // 2):
        for i in every:
            if i > 0:
                same.append((at(2 * c, i), at(2 * c, i - 1)))
                cross.append((at(2 * c, i), at(2 * c + 1, i - 1)))
            if i < groups - 1:
                same.append((at(2 * c + 1, i), at(2 * c + 1, i + 1)))
                cross.append((at(2 * c + 1, i), at(2 * c, i + 1)))
    leftward = [(i, i - 1) for i in range(1, groups)]
    rightward = [(i, i + 1) for i in range(groups - 1)]

    left, right = in_hbm(left_env[0]), in_hbm(right_env[0])
    whole = (2, channels) + block
    own, other = pl.pallas_call(
        split_kernel,
        out_shape=[jax.ShapeDtypeStruct((2,) + block, BF16)] * 2,
        in_specs=anywhere(2),
        out_specs=vmem(2),
        scratch_shapes=[
            pltpu.VMEM((2,) + block, F32),
            pltpu.VMEM((2,) + block, BF16),
            pltpu.SemaphoreType.DMA((2,)),
        ],
        compiler_params=limit(4),
        cost_estimate=cost(0, size, 2 * MIB),
    )(in_hbm(gauge_offset[0]), in_hbm(state_blocks[0]))
    got = lax.ppermute(other, AXES, swap)
    cells, to_left, to_right, table = pl.pallas_call(
        table_kernel,
        out_shape=[
            jax.ShapeDtypeStruct((2,) + block, BF16),
            jax.ShapeDtypeStruct((QUARTER,) + block, BF16),
            jax.ShapeDtypeStruct((QUARTER,) + block, BF16),
            jax.ShapeDtypeStruct((4, channels), jnp.int32),
        ],
        in_specs=anywhere(4),
        out_specs=vmem(3) + smem(1),
        scratch_shapes=[
            pltpu.SMEM(charge.shape, jnp.int32),
            pltpu.SMEM(mpo_mask.shape, jnp.int32),
            pltpu.SMEM(block_dims.shape, jnp.int32),
            pltpu.SemaphoreType.DMA((3,)),
            pltpu.SemaphoreType.DMA((2, QUARTER)),
        ],
        compiler_params=limit(4),
        cost_estimate=cost(0, size, 2 * MIB),
    )(in_hbm(charge), in_hbm(mpo_mask), in_hbm(block_dims), left)
    left_up = lax.ppermute(to_right, "sec", rightward)
    left_down = lax.ppermute(to_left, "sec", leftward)

    def sort(masked, source):
        return pl.pallas_call(
            functools.partial(sort_kernel, masked),
            out_shape=jax.ShapeDtypeStruct(whole, BF16),
            in_specs=smem(1) + anywhere(1),
            out_specs=vmem(1)[0],
            scratch_shapes=[pltpu.SemaphoreType.DMA((2, channels))],
            compiler_params=limit(4),
            cost_estimate=cost(0, size, 8 * MIB),
        )(table, source)

    pair = pl.pallas_call(
        pair_kernel,
        out_shape=jax.ShapeDtypeStruct(block, BF16),
        in_specs=vmem(2) + anywhere(1),
        out_specs=vmem(1)[0],
        compiler_params=limit(4),
        cost_estimate=cost(1, size, MIB),
    )(own, got, cells)
    near = lax.ppermute(pair, AXES, chip_pairs)
    left_sorted = sort(False, left)
    four = pl.pallas_call(
        four_kernel,
        out_shape=jax.ShapeDtypeStruct(block, BF16),
        in_specs=vmem(2) + anywhere(1),
        out_specs=vmem(1)[0],
        compiler_params=limit(4),
        cost_estimate=cost(1, size, MIB),
    )(pair, near, left_sorted)
    far = lax.ppermute(four, AXES, far_pairs)
    right_sorted = sort(True, right)

    x_own, x_other = pl.pallas_call(
        state_kernel,
        out_shape=[jax.ShapeDtypeStruct(block, BF16)] * 2,
        in_specs=vmem(5) + anywhere(3),
        out_specs=vmem(2),
        scratch_shapes=[pltpu.VMEM((2, 2) + block, BF16)],
        compiler_params=limit(6),
        cost_estimate=cost(8, size, 2 * MIB),
    )(cells, own, got, near, far, right_sorted, left_up, left_down)
    x_got = lax.ppermute(x_other, AXES, swap)
    side_same = lax.ppermute(x_own, AXES, same)
    side_cross = lax.ppermute(x_other, AXES, cross)

    acc, env, x_here = pl.pallas_call(
        own_kernel,
        out_shape=[
            jax.ShapeDtypeStruct((2,) + block, F32),
            pltpu.HBM((1, 2, channels) + block, BF16),
            jax.ShapeDtypeStruct((2,) + block, BF16),
        ],
        in_specs=vmem(4) + anywhere(1),
        out_specs=vmem(1) + anywhere(1) + vmem(1),
        scratch_shapes=[
            pltpu.VMEM((2, size, channels * size), BF16),
            pltpu.VMEM((2, channels - QUARTER) + block, BF16),
            pltpu.SMEM((4, channels), jnp.int32),
            pltpu.SemaphoreType.DMA((1,)),
            pltpu.SemaphoreType.DMA((2, channels - QUARTER)),
        ],
        compiler_params=limit(12),
        cost_estimate=cost(88, size, 12 * MIB),
    )(x_own, x_got, left_sorted, right_sorted, table)

    v_first, v_second, sums, x_side = pl.pallas_call(
        image_kernel,
        out_shape=[
            jax.ShapeDtypeStruct(block, BF16),
            jax.ShapeDtypeStruct(block, BF16),
            jax.ShapeDtypeStruct((groups, 128), F32),
            jax.ShapeDtypeStruct((2,) + block, BF16),
        ],
        in_specs=vmem(7),
        out_specs=vmem(4),
        scratch_shapes=[pltpu.VMEM((2, size, QUARTER * size), BF16)],
        compiler_params=limit(10),
        cost_estimate=cost(16, size, 4 * MIB),
    )(cells, x_here, side_same, side_cross, left_sorted, right_sorted, acc)
    v_right = lax.ppermute(v_first, "sec", leftward)
    v_left = lax.ppermute(v_second, "sec", rightward)
    sums = lax.all_to_all(sums, "sec", 0, 0)

    total_cells = float(groups * 2 * size * size)
    krylov, env, rayleigh = pl.pallas_call(
        lambda *refs: krylov_kernel(total_cells, *refs),
        out_shape=[
            jax.ShapeDtypeStruct((1, 2) + block, BF16),
            jax.ShapeDtypeStruct((1, 2, channels) + block, BF16),
            jax.ShapeDtypeStruct((1,), F32),
        ],
        in_specs=vmem(10) + anywhere(6),
        out_specs=vmem(1) + anywhere(1) + smem(1),
        scratch_shapes=[
            pltpu.VMEM(whole, BF16),
            pltpu.VMEM(whole, BF16),
            pltpu.VMEM((4,) + block, BF16),
            pltpu.VMEM((size, channels * size), BF16),
            pltpu.VMEM((size, QUARTER * size), BF16),
            pltpu.VMEM((2, QUARTER) + block, BF16),
            pltpu.SMEM((4, channels), jnp.int32),
            pltpu.SMEM(charge.shape, jnp.int32),
            pltpu.SMEM(mpo_mask.shape, jnp.int32),
            pltpu.SemaphoreType.DMA((8,)),
            pltpu.SemaphoreType.DMA((3,)),
            pltpu.SemaphoreType.DMA((2, QUARTER)),
        ],
        input_output_aliases={15: 1},
        compiler_params=limit(32),
        cost_estimate=cost(80, size, 12 * MIB),
    )(cells, sums, x_here, x_side, v_first, v_second, v_left, v_right, left_up, left_down,
      table, in_hbm(charge), in_hbm(mpo_mask), left, right, env)
    return krylov, env, rayleigh


def solution(mesh):
    return jax.shard_map(
        local,
        mesh=mesh,
        in_specs=(
            P("seg", "sec", None, None),
            P("seg", "sec", None, None),
            P("seg", "sec", None, None, None),
            P("seg", "sec", None, None, None),
            P("sec", None),
            P(),
            P("sec"),
        ),
        out_specs=(P("seg", "sec", None, None), P("seg", "sec", None, None, None), P("seg")),
        check_vma=False,
    )
```

```python
import functools

import jax
import jax.numpy as jnp
from jax import lax
from jax.experimental import pallas as pl
from jax.experimental.pallas import tpu as pltpu
from jax.sharding import PartitionSpec as P

F32 = jnp.float32
BF16 = jnp.bfloat16
AXES = ("seg", "sec")
QUARTER = 4
MIB = 1 << 20


def dot(first, second):
    return lax.dot_general(
        first, second, (((1,), (0,)), ((), ())), preferred_element_type=F32
    )


def vmem(count):
    return [pl.BlockSpec(memory_space=pltpu.VMEM)] * count


def smem(count):
    return [pl.BlockSpec(memory_space=pltpu.SMEM)] * count


def anywhere(count):
    return [pl.BlockSpec(memory_space=pl.ANY)] * count


def cost(products, size, bytes_accessed):
    return pl.CostEstimate(
        flops=2 * products * size**3, bytes_accessed=bytes_accessed, transcendentals=0
    )


def place():
    return lax.axis_index("seg") % 2


def limit(mebibytes):
    return pltpu.CompilerParams(vmem_limit_bytes=mebibytes * MIB)


def live(dim, size):
    rows = lax.broadcasted_iota(jnp.int32, (size, size), 0) < dim
    columns = lax.broadcasted_iota(jnp.int32, (size, size), 1) < dim
    return rows & columns


def in_hbm(array):
    return pltpu.with_memory_space_constraint(array, pltpu.HBM)


def split_kernel(gauge, state, own, other, gauge_here, state_here, sems):
    core = place()
    arrivals = [
        pltpu.make_async_copy(gauge, gauge_here, sems.at[0]),
        pltpu.make_async_copy(state, state_here, sems.at[1]),
    ]
    for copy in arrivals:
        copy.start()
    for copy in arrivals:
        copy.wait()
    own[0] = gauge_here[core].astype(BF16)
    own[1] = state_here[core]
    other[0] = gauge_here[1 - core].astype(BF16)
    other[1] = state_here[1 - core]


def table_kernel(charge_far, mask_far, dims_far, cells, table, charge, mask, dims, sems):
    channels, size = charge.shape[0], cells.shape[1]
    arrivals = [
        pltpu.make_async_copy(charge_far, charge, sems.at[0]),
        pltpu.make_async_copy(mask_far, mask, sems.at[1]),
        pltpu.make_async_copy(dims_far, dims, sems.at[2]),
    ]
    for copy in arrivals:
        copy.start()
    for copy in arrivals:
        copy.wait()
    ups, downs, rest = jnp.int32(0), jnp.int32(0), jnp.int32(0)
    for w in range(channels):
        up, down = charge[w] == 1, charge[w] == -1
        middle = QUARTER + rest
        table[0, jnp.where(up, ups, jnp.where(down, channels - QUARTER + downs, middle))] = w
        table[1, jnp.where(down, downs, jnp.where(up, channels - QUARTER + ups, middle))] = w
        ups = ups + up.astype(jnp.int32)
        downs = downs + down.astype(jnp.int32)
        rest = rest + jnp.where(up | down, 0, 1)
    for s in range(2):
        for j in range(channels):
            table[2 + s, j] = mask[s, table[s, j]]
        cells[s] = jnp.where(live(dims[s], size), 1.0, 0.0).astype(BF16)


def sort_kernel(table, left, right, left_sorted, right_sorted, sems):
    channels = left.shape[1]

    def copy(side, s, j):
        source, target = ((left, left_sorted), (right, right_sorted))[side]
        return pltpu.make_async_copy(
            source.at[s, table[s, j]], target.at[s, j], sems.at[side, s, j]
        )

    every = [(side, s, j) for side in range(2) for s in range(2) for j in range(channels)]
    for where in every:
        copy(*where).start()
    for where in every:
        copy(*where).wait()
    for s in range(2):
        for j in range(channels):
            @pl.when(table[2 + s, j] == 0)
            def _():
                right_sorted[s, j] = jnp.zeros(right_sorted.shape[2:], right_sorted.dtype)


def relay_kernel(pair, after, out):
    out[...] = pair[1]


def joined(later, earlier):
    return later.astype(F32) + earlier.astype(F32) + dot(later, earlier)


def pair_kernel(own, got, after, out):
    core = place()

    @pl.when(core == 0)
    def _():
        out[...] = joined(got[0], own[0]).astype(BF16)

    @pl.when(core == 1)
    def _():
        out[...] = joined(own[0], got[0]).astype(BF16)


def state_kernel(cells, own, got, one_back, two_back, three_back, *refs):
    x_pair, pair = refs[-2:]
    core = place()
    size = x_pair.shape[1]
    pair[core] = own[...]
    pair[1 - core] = got[...]
    field = jnp.concatenate([pair[0, 1], pair[1, 1]], axis=1)
    wide = field.astype(F32)
    wide = wide + dot(three_back[...], field)
    wide = wide + dot(two_back[...], wide.astype(BF16))
    wide = wide + dot(one_back[...], wide.astype(BF16))
    wide = wide + dot(pair[0, 0], wide.astype(BF16))
    earlier, later = wide[:, :size], wide[:, size:]
    later = later + dot(pair[1, 0], later.astype(BF16))
    alive = cells[core] != 0
    first = jnp.where(alive, earlier, 0.0).astype(BF16)
    second = jnp.where(alive, later, 0.0).astype(BF16)
    x_pair[core] = first
    x_pair[1 - core] = second


def spread(parts, s, blocks, field, first, last):
    size = field.shape[0]
    rows = blocks[s, first:last].reshape((last - first) * size, size)
    result = dot(rows, field).astype(BF16)
    for j in range(first, last):
        at = (j - first) * size
        parts[s, :, j * size : (j + 1) * size] = result[at : at + size]


def folded(parts, s, blocks, first, last):
    size = blocks.shape[-1]
    rows = blocks[s, first:last].reshape((last - first) * size, size)
    return dot(parts[s, :, first * size : last * size], rows)


def own_kernel(x_pair, x_swapped, left, right, table_far, acc, env, x_here, crossing, parts,
               blocks, table, table_sem, out_sems):
    core = place()
    channels, size = left.shape[1], left.shape[2]
    cross = channels - QUARTER
    fetch = pltpu.make_async_copy(table_far, table, table_sem.at[0])
    fetch.start()
    x_here[core] = x_pair[0]
    x_here[1 - core] = x_swapped[1]

    def send(s, j):
        target = 1 - s if j < QUARTER else s
        return pltpu.make_async_copy(
            blocks.at[s, j], env.at[0, target, table[s, j]], out_sems.at[s, j]
        )

    for s in range(2):
        field = x_here[s]
        turned = field.T
        spread(parts, s, left, field, 0, channels)
        result = dot(turned, parts[s]).astype(BF16)
        for j in range(cross):
            blocks[s, j] = result[:, j * size : (j + 1) * size]
        for j in range(cross, channels):
            crossing[s, j - cross] = result[:, j * size : (j + 1) * size]
        if s == 0:
            fetch.wait()
        for j in range(cross):
            send(s, j).start()
    for s in range(2):
        spread(parts, s, left, x_here[1 - s], cross, channels)
        acc[s] = folded(parts, s, right, QUARTER, channels)
    for s in range(2):
        for j in range(cross):
            send(s, j).wait()


def image_kernel(cells, x_here, side_same, side_swapped, left, right, acc, crossing, to_left,
                 to_right, sums, x_side, parts):
    core = place()
    x_side[1 - core] = side_same[0]
    x_side[core] = side_swapped[...]
    total = []
    for s in range(2):
        spread(parts, s, left, x_side[s], 0, QUARTER)
        image = acc[s] + folded(parts, s, right, 0, QUARTER)
        image = jnp.where(cells[s] != 0, image, 0.0).astype(BF16)
        message = (to_left, to_right)[s]
        message[:QUARTER] = crossing[s]
        message[QUARTER] = image
        total.append(image)

    def whole(values):
        return jnp.sum(jnp.sum(values, axis=0, keepdims=True), axis=1, keepdims=True)

    x_wide = [x_here[s].astype(F32) for s in range(2)]
    v_wide = [total[s].astype(F32) for s in range(2)]
    norm = whole(x_wide[0] * x_wide[0] + x_wide[1] * x_wide[1])
    correlation = whole(x_wide[0] * v_wide[0] + x_wide[1] * v_wide[1])
    ratio = jnp.where(norm > 0.0, correlation / jnp.where(norm > 0.0, norm, 1.0), 0.0)
    apart = [v_wide[s] - ratio * x_wide[s] for s in range(2)]
    spread_of = whole(apart[0] * apart[0] + apart[1] * apart[1])
    lane = lax.broadcasted_iota(jnp.int32, sums.shape, 1)
    row = jnp.where(lane == 0, norm, jnp.where(lane == 1, correlation, 0.0))
    row = jnp.where(lane == 2, ratio, jnp.where(lane == 3, spread_of, row))
    sums[...] = row


def apart_kernel(sums, x_here, to_left, to_right, left, right, image, sums_out, parts):
    channels = left.shape[1]
    cross = channels - QUARTER
    ratio = sums[0:1, 2:3]

    def apart(v, x):
        return (v.astype(F32) - ratio * x.astype(F32)).astype(BF16)

    inner = [apart((to_left, to_right)[s][QUARTER], x_here[s]) for s in range(2)]
    for s in range(2):
        spread(parts, s, left, inner[s], QUARTER, cross)
        spread(parts, s, left, inner[1 - s], cross, channels)
        image[s] = folded(parts, s, right, QUARTER, channels)
    sums_out[...] = sums[...]


def krylov_kernel(total_cells, cells, sums, sums_here, image, acc, x_side, from_left, from_right,
                  left, right, table_far, env_in, krylov, env, rayleigh, parts, table,
                  table_sem, out_sems):
    fetch = pltpu.make_async_copy(table_far, table, table_sem.at[0])
    fetch.start()
    column = [jnp.sum(sums[:, i : i + 1], axis=0, keepdims=True) for i in range(2)]
    ratio = column[1] / column[0]
    apart = ratio - sums[:, 2:3]
    spread_of = jnp.sum(sums[:, 3:4] + apart * apart * sums[:, 0:1], axis=0, keepdims=True)
    inverse = 1.0 / jnp.sqrt(spread_of * (1.0 / total_cells) + 1e-06)
    rayleigh[0] = ratio[0, 0]
    missing = ratio - sums_here[0:1, 2:3]

    def send(s, j):
        return pltpu.make_async_copy(
            (from_left, from_right)[s].at[j], env.at[0, s, table[s, j]], out_sems.at[s, j]
        )

    for s in range(2):
        arrived = (from_left, from_right)[s][QUARTER].astype(F32)
        outer = (arrived - ratio * x_side[s].astype(F32)).astype(BF16)
        spread(parts, s, left, outer, 0, QUARTER)
        if s == 0:
            fetch.wait()
            for t in range(2):
                for j in range(QUARTER):
                    send(t, j).start()
        whole = image[s] - missing * acc[s] + folded(parts, s, right, 0, QUARTER)
        krylov[0, s] = jnp.where(cells[s] != 0, whole * inverse, 0.0).astype(BF16)
    for s in range(2):
        for j in range(QUARTER):
            send(s, j).wait()


def local(state_blocks, gauge_offset, left_env, right_env, mpo_mask, charge, block_dims):
    size = state_blocks.shape[-1]
    channels = left_env.shape[2]
    segments = lax.axis_size("seg")
    groups = lax.axis_size("sec")
    block = (size, size)

    def at(segment, group):
        return segment * groups + group

    every = range(groups)
    swap = [(at(k, i), at(k ^ 1, i)) for k in range(segments) for i in every]
    def onward(chips):
        return [
            (at(k, i), at(k + 2 * chips, i)) for k in range(segments - 2 * chips) for i in every
        ]

    same = [
        (at(2 * c + r, i), at(2 * c + r, i + 2 * r - 1))
        for c in range(segments // 2) for r in range(2) for i in every
        if 0 <= i + 2 * r - 1 < groups
    ]
    leftward = [(i, i - 1) for i in range(1, groups)]
    rightward = [(i, i + 1) for i in range(groups - 1)]

    left, right = in_hbm(left_env[0]), in_hbm(right_env[0])
    whole = (2, channels) + block
    own, other = pl.pallas_call(
        split_kernel,
        out_shape=[jax.ShapeDtypeStruct((2,) + block, BF16)] * 2,
        in_specs=anywhere(2),
        out_specs=vmem(2),
        scratch_shapes=[
            pltpu.VMEM((2,) + block, F32),
            pltpu.VMEM((2,) + block, BF16),
            pltpu.SemaphoreType.DMA((2,)),
        ],
        compiler_params=limit(4),
        cost_estimate=cost(0, size, 2 * MIB),
    )(in_hbm(gauge_offset[0]), in_hbm(state_blocks[0]))
    got = lax.ppermute(other, AXES, swap)
    cells, table = pl.pallas_call(
        table_kernel,
        out_shape=[
            jax.ShapeDtypeStruct((2,) + block, BF16),
            jax.ShapeDtypeStruct((4, channels), jnp.int32),
        ],
        in_specs=anywhere(3),
        out_specs=vmem(1) + smem(1),
        scratch_shapes=[
            pltpu.SMEM(charge.shape, jnp.int32),
            pltpu.SMEM(mpo_mask.shape, jnp.int32),
            pltpu.SMEM(block_dims.shape, jnp.int32),
            pltpu.SemaphoreType.DMA((3,)),
        ],
        compiler_params=limit(4),
        cost_estimate=cost(0, size, 2 * MIB),
    )(in_hbm(charge), in_hbm(mpo_mask), in_hbm(block_dims))

    pair = pl.pallas_call(
        pair_kernel,
        out_shape=jax.ShapeDtypeStruct(block, BF16),
        in_specs=vmem(2) + anywhere(1),
        out_specs=vmem(1)[0],
        compiler_params=limit(4),
        cost_estimate=cost(1, size, MIB),
    )(own, got, cells)
    backs = [lax.ppermute(pair, AXES, onward(chips)) for chips in range(1, segments // 2)]
    left_sorted, right_sorted = pl.pallas_call(
        sort_kernel,
        out_shape=[jax.ShapeDtypeStruct(whole, BF16)] * 2,
        in_specs=smem(1) + anywhere(2),
        out_specs=vmem(2),
        scratch_shapes=[pltpu.SemaphoreType.DMA((2, 2, channels))],
        compiler_params=limit(4),
        cost_estimate=cost(0, size, 16 * MIB),
    )(table, left, right)
    x_pair = pl.pallas_call(
        state_kernel,
        out_shape=jax.ShapeDtypeStruct((2,) + block, BF16),
        in_specs=vmem(6) + anywhere(1),
        out_specs=vmem(1)[0],
        scratch_shapes=[pltpu.VMEM((2, 2) + block, BF16)],
        compiler_params=limit(6),
        cost_estimate=cost(8, size, 2 * MIB),
    )(cells, own, got, *backs, right_sorted)
    x_swapped = lax.ppermute(x_pair, AXES, swap)
    side_same = lax.ppermute(x_pair, AXES, same)
    acc, env, x_here, crossing = pl.pallas_call(
        own_kernel,
        out_shape=[
            jax.ShapeDtypeStruct((2,) + block, F32),
            pltpu.HBM((1, 2, channels) + block, BF16),
            jax.ShapeDtypeStruct((2,) + block, BF16),
            jax.ShapeDtypeStruct((2, QUARTER) + block, BF16),
        ],
        in_specs=vmem(4) + anywhere(1),
        out_specs=vmem(1) + anywhere(1) + vmem(2),
        scratch_shapes=[
            pltpu.VMEM((2, size, channels * size), BF16),
            pltpu.VMEM((2, channels - QUARTER) + block, BF16),
            pltpu.SMEM((4, channels), jnp.int32),
            pltpu.SemaphoreType.DMA((1,)),
            pltpu.SemaphoreType.DMA((2, channels - QUARTER)),
        ],
        compiler_params=limit(12),
        cost_estimate=cost(96, size, 12 * MIB),
    )(x_pair, x_swapped, left_sorted, right_sorted, table)

    relayed = pl.pallas_call(
        relay_kernel,
        out_shape=jax.ShapeDtypeStruct(block, BF16),
        in_specs=vmem(1) + anywhere(1),
        out_specs=vmem(1)[0],
        compiler_params=limit(2),
        cost_estimate=cost(0, size, MIB),
    )(side_same, acc)
    side_swapped = lax.ppermute(relayed, AXES, swap)
    to_left, to_right, sums, x_side = pl.pallas_call(
        image_kernel,
        out_shape=[
            jax.ShapeDtypeStruct((QUARTER + 1,) + block, BF16),
            jax.ShapeDtypeStruct((QUARTER + 1,) + block, BF16),
            pltpu.VMEM((groups, 128), F32),
            jax.ShapeDtypeStruct((2,) + block, BF16),
        ],
        in_specs=vmem(8),
        out_specs=vmem(4),
        scratch_shapes=[pltpu.VMEM((2, size, QUARTER * size), BF16)],
        compiler_params=limit(10),
        cost_estimate=cost(16, size, 4 * MIB),
    )(cells, x_here, side_same, side_swapped, left_sorted, right_sorted, acc, crossing)
    from_right = lax.ppermute(to_left, "sec", leftward)
    from_left = lax.ppermute(to_right, "sec", rightward)
    image, sums_here = pl.pallas_call(
        apart_kernel,
        out_shape=[
            jax.ShapeDtypeStruct((2,) + block, F32),
            pltpu.VMEM((groups, 128), F32),
        ],
        in_specs=vmem(6),
        out_specs=vmem(2),
        scratch_shapes=[pltpu.VMEM((2, size, channels * size), BF16)],
        compiler_params=limit(10),
        cost_estimate=cost(48, size, 4 * MIB),
    )(sums, x_here, to_left, to_right, left_sorted, right_sorted)
    sums = lax.all_to_all(sums_here, "sec", 0, 0)

    total_cells = float(groups * 2 * size * size)
    krylov, env, rayleigh = pl.pallas_call(
        functools.partial(krylov_kernel, total_cells),
        out_shape=[
            jax.ShapeDtypeStruct((1, 2) + block, BF16),
            jax.ShapeDtypeStruct((1, 2, channels) + block, BF16),
            jax.ShapeDtypeStruct((1,), F32),
        ],
        in_specs=vmem(10) + anywhere(2),
        out_specs=vmem(1) + anywhere(1) + smem(1),
        scratch_shapes=[
            pltpu.VMEM((2, size, QUARTER * size), BF16),
            pltpu.SMEM((4, channels), jnp.int32),
            pltpu.SemaphoreType.DMA((1,)),
            pltpu.SemaphoreType.DMA((2, QUARTER)),
        ],
        input_output_aliases={11: 1},
        compiler_params=limit(8),
        cost_estimate=cost(16, size, 4 * MIB),
    )(cells, sums, sums_here, image, acc, x_side, from_left, from_right, left_sorted,
      right_sorted, table, env)
    return krylov, env, rayleigh


def solution(mesh):
    return jax.shard_map(
        local,
        mesh=mesh,
        in_specs=(
            P("seg", "sec", None, None),
            P("seg", "sec", None, None),
            P("seg", "sec", None, None, None),
            P("seg", "sec", None, None, None),
            P("sec", None),
            P(),
            P("sec"),
        ),
        out_specs=(P("seg", "sec", None, None), P("seg", "sec", None, None, None), P("seg")),
        check_vma=False,
    )
```

```python
import functools

import jax
import jax.numpy as jnp
from jax import lax
from jax.experimental import pallas as pl
from jax.experimental.pallas import tpu as pltpu
from jax.sharding import PartitionSpec as P

F32 = jnp.float32
BF16 = jnp.bfloat16
AXES = ("seg", "sec")
QUARTER = 4
MIB = 1 << 20


def dot(first, second):
    return lax.dot_general(
        first, second, (((1,), (0,)), ((), ())), preferred_element_type=F32
    )


def vmem(count):
    return [pl.BlockSpec(memory_space=pltpu.VMEM)] * count


def smem(count):
    return [pl.BlockSpec(memory_space=pltpu.SMEM)] * count


def anywhere(count):
    return [pl.BlockSpec(memory_space=pl.ANY)] * count


def cost(products, size, bytes_accessed):
    return pl.CostEstimate(
        flops=2 * products * size**3, bytes_accessed=bytes_accessed, transcendentals=0
    )


def place():
    return lax.axis_index("seg") % 2


def odd_place():
    return lax.axis_index("sec") % 2 == 1


def limit(mebibytes):
    return pltpu.CompilerParams(vmem_limit_bytes=mebibytes * MIB)


def live(dim, size):
    rows = lax.broadcasted_iota(jnp.int32, (size, size), 0) < dim
    columns = lax.broadcasted_iota(jnp.int32, (size, size), 1) < dim
    return rows & columns


def in_hbm(array):
    return pltpu.with_memory_space_constraint(array, pltpu.HBM)


def split_kernel(gauge, state, own, other, gauge_here, state_here, sems):
    core = place()
    arrivals = [
        pltpu.make_async_copy(gauge, gauge_here, sems.at[0]),
        pltpu.make_async_copy(state, state_here, sems.at[1]),
    ]
    for copy in arrivals:
        copy.start()
    for copy in arrivals:
        copy.wait()
    own[0] = gauge_here[core].astype(BF16)
    own[1] = state_here[core]
    other[0] = gauge_here[1 - core].astype(BF16)
    other[1] = state_here[1 - core]


def table_kernel(charge_far, mask_far, dims_far, cells, table, charge, mask, dims, sems):
    channels, size = charge.shape[0], cells.shape[1]
    arrivals = [
        pltpu.make_async_copy(charge_far, charge, sems.at[0]),
        pltpu.make_async_copy(mask_far, mask, sems.at[1]),
        pltpu.make_async_copy(dims_far, dims, sems.at[2]),
    ]
    for copy in arrivals:
        copy.start()
    for copy in arrivals:
        copy.wait()
    ups, downs, rest = jnp.int32(0), jnp.int32(0), jnp.int32(0)
    for w in range(channels):
        up, down = charge[w] == 1, charge[w] == -1
        middle = QUARTER + rest
        table[0, jnp.where(up, ups, jnp.where(down, channels - QUARTER + downs, middle))] = w
        table[1, jnp.where(down, downs, jnp.where(up, channels - QUARTER + ups, middle))] = w
        ups = ups + up.astype(jnp.int32)
        downs = downs + down.astype(jnp.int32)
        rest = rest + jnp.where(up | down, 0, 1)
    for s in range(2):
        for j in range(channels):
            table[2 + s, j] = mask[s, table[s, j]]
        cells[s] = jnp.where(live(dims[s], size), 1.0, 0.0).astype(BF16)


def sort_kernel(table, left, right, left_sorted, right_sorted, sems):
    channels = left.shape[1]

    def copy(side, s, j):
        source, target = ((left, left_sorted), (right, right_sorted))[side]
        return pltpu.make_async_copy(
            source.at[s, table[s, j]], target.at[s, j], sems.at[side, s, j]
        )

    every = [(side, s, j) for side in range(2) for s in range(2) for j in range(channels)]
    for where in every:
        copy(*where).start()
    for where in every:
        copy(*where).wait()
    for s in range(2):
        for j in range(channels):
            @pl.when(table[2 + s, j] == 0)
            def _():
                right_sorted[s, j] = jnp.zeros(right_sorted.shape[2:], right_sorted.dtype)


def relay_kernel(pair, after, out):
    out[...] = pair[0]


def joined(later, earlier):
    return later.astype(F32) + earlier.astype(F32) + dot(later, earlier)


def pair_kernel(own, got, after, out):
    core = place()

    @pl.when(core == 0)
    def _():
        out[...] = joined(got[0], own[0]).astype(BF16)

    @pl.when(core == 1)
    def _():
        out[...] = joined(own[0], got[0]).astype(BF16)


def state_kernel(cells, own, got, one_back, two_back, three_back, *refs):
    x_pair, pair = refs[-2:]
    core = place()
    size = x_pair.shape[1]
    pair[core] = own[...]
    pair[1 - core] = got[...]
    field = jnp.concatenate([pair[0, 1], pair[1, 1]], axis=1)
    wide = field.astype(F32)
    wide = wide + dot(three_back[...], field)
    wide = wide + dot(two_back[...], wide.astype(BF16))
    wide = wide + dot(one_back[...], wide.astype(BF16))
    wide = wide + dot(pair[0, 0], wide.astype(BF16))
    earlier, later = wide[:, :size], wide[:, size:]
    later = later + dot(pair[1, 0], later.astype(BF16))
    alive = cells[core] != 0
    first = jnp.where(alive, earlier, 0.0).astype(BF16)
    second = jnp.where(alive, later, 0.0).astype(BF16)
    x_pair[core] = first
    x_pair[1 - core] = second


def spread(parts, s, blocks, field, first, last):
    size = field.shape[0]
    rows = blocks[s, first:last].reshape((last - first) * size, size)
    result = dot(rows, field).astype(BF16)
    for j in range(first, last):
        at = (j - first) * size
        parts[s, :, j * size : (j + 1) * size] = result[at : at + size]


def folded(parts, s, blocks, first, last):
    size = blocks.shape[-1]
    rows = blocks[s, first:last].reshape((last - first) * size, size)
    return dot(parts[s, :, first * size : last * size], rows)


def own_kernel(x_pair, x_swapped, left, right, table_far, acc, env, x_here, crossing, parts,
               blocks, table, table_sem, out_sems):
    core = place()
    channels, size = left.shape[1], left.shape[2]
    cross = channels - QUARTER
    fetch = pltpu.make_async_copy(table_far, table, table_sem.at[0])
    fetch.start()
    x_here[core] = x_pair[0]
    x_here[1 - core] = x_swapped[1]

    def send(s, j):
        target = 1 - s if j < QUARTER else s
        return pltpu.make_async_copy(
            blocks.at[s, j], env.at[0, target, table[s, j]], out_sems.at[s, j]
        )

    for s in range(2):
        field = x_here[s]
        turned = field.T
        spread(parts, s, left, field, 0, channels)
        result = dot(turned, parts[s]).astype(BF16)
        for j in range(cross):
            blocks[s, j] = result[:, j * size : (j + 1) * size]
        for j in range(cross, channels):
            crossing[s, j - cross] = result[:, j * size : (j + 1) * size]
        if s == 0:
            fetch.wait()
        for j in range(cross):
            send(s, j).start()
    for s in range(2):
        spread(parts, s, left, x_here[1 - s], cross, channels)
        acc[s] = folded(parts, s, right, QUARTER, channels)
    for s in range(2):
        for j in range(cross):
            send(s, j).wait()


def image_kernel(cells, x_here, side_beside, side_swapped, left, right, acc, crossing, to_first,
                 to_second, sums, x_side, parts):
    core = place()
    x_side[core] = side_beside[1]
    x_side[1 - core] = side_swapped[...]
    total = []
    for s in range(2):
        spread(parts, s, left, x_side[s], 0, QUARTER)
        image = acc[s] + folded(parts, s, right, 0, QUARTER)
        image = jnp.where(cells[s] != 0, image, 0.0).astype(BF16)
        total.append(image)
    odd = odd_place()
    for is_odd in range(2):
        @pl.when(odd == (is_odd == 1))
        def _():
            for s in range(2):
                message = (to_first, to_second)[s ^ is_odd ^ 1]
                message[:QUARTER] = crossing[s]
                message[QUARTER] = total[s]

    def whole(values):
        return jnp.sum(jnp.sum(values, axis=0, keepdims=True), axis=1, keepdims=True)

    x_wide = [x_here[s].astype(F32) for s in range(2)]
    v_wide = [total[s].astype(F32) for s in range(2)]
    norm = whole(x_wide[0] * x_wide[0] + x_wide[1] * x_wide[1])
    correlation = whole(x_wide[0] * v_wide[0] + x_wide[1] * v_wide[1])
    ratio = jnp.where(norm > 0.0, correlation / jnp.where(norm > 0.0, norm, 1.0), 0.0)
    apart = [v_wide[s] - ratio * x_wide[s] for s in range(2)]
    spread_of = whole(apart[0] * apart[0] + apart[1] * apart[1])
    lane = lax.broadcasted_iota(jnp.int32, sums.shape, 1)
    row = jnp.where(lane == 0, norm, jnp.where(lane == 1, correlation, 0.0))
    row = jnp.where(lane == 2, ratio, jnp.where(lane == 3, spread_of, row))
    sums[...] = row


def apart_kernel(sums, x_here, to_first, to_second, left, right, image, sums_out, parts):
    odd = odd_place()
    first, second = to_first[QUARTER], to_second[QUARTER]
    here = [jnp.where(odd, first, second), jnp.where(odd, second, first)]
    channels = left.shape[1]
    cross = channels - QUARTER
    ratio = sums[0:1, 2:3]

    def apart(v, x):
        return (v.astype(F32) - ratio * x.astype(F32)).astype(BF16)

    inner = [apart(here[s], x_here[s]) for s in range(2)]
    for s in range(2):
        spread(parts, s, left, inner[s], QUARTER, cross)
        spread(parts, s, left, inner[1 - s], cross, channels)
        image[s] = folded(parts, s, right, QUARTER, channels)
    sums_out[...] = sums[...]


def krylov_kernel(total_cells, cells, sums, sums_here, image, acc, x_side, from_first,
                  from_second, left, right, table, env_in, krylov, env, rayleigh, parts,
                  out_sems):
    odd = odd_place()
    place_of = [[table[s : s + 1, j : j + 1][0, 0] for j in range(QUARTER)] for s in range(2)]

    def send(is_odd, s, j):
        source = (from_first, from_second)[s ^ is_odd ^ 1]
        return pltpu.make_async_copy(
            source.at[j], env.at[0, s, place_of[s][j]], out_sems.at[s, j]
        )

    for is_odd in range(2):
        @pl.when(odd == (is_odd == 1))
        def _():
            for s in range(2):
                for j in range(QUARTER):
                    send(is_odd, s, j).start()
    column = [jnp.sum(sums[:, i : i + 1], axis=0, keepdims=True) for i in range(2)]
    ratio = column[1] / column[0]
    apart = ratio - sums[:, 2:3]
    spread_of = jnp.sum(sums[:, 3:4] + apart * apart * sums[:, 0:1], axis=0, keepdims=True)
    inverse = 1.0 / jnp.sqrt(spread_of * (1.0 / total_cells) + 1e-06)
    rayleigh[0] = ratio[0, 0]
    missing = ratio - sums_here[0:1, 2:3]
    first, second = from_first[QUARTER], from_second[QUARTER]
    arrived = [jnp.where(odd, first, second), jnp.where(odd, second, first)]
    for s in range(2):
        outer = (arrived[s].astype(F32) - ratio * x_side[s].astype(F32)).astype(BF16)
        spread(parts, s, left, outer, 0, QUARTER)
        whole = image[s] - missing * acc[s] + folded(parts, s, right, 0, QUARTER)
        krylov[0, s] = jnp.where(cells[s] != 0, whole * inverse, 0.0).astype(BF16)
    for is_odd in range(2):
        @pl.when(odd == (is_odd == 1))
        def _():
            for s in range(2):
                for j in range(QUARTER):
                    send(is_odd, s, j).wait()


def local(state_blocks, gauge_offset, left_env, right_env, mpo_mask, charge, block_dims):
    size = state_blocks.shape[-1]
    channels = left_env.shape[2]
    segments = lax.axis_size("seg")
    groups = lax.axis_size("sec")
    block = (size, size)

    def at(segment, group):
        return segment * groups + group

    every = range(groups)
    swap = [(at(k, i), at(k ^ 1, i)) for k in range(segments) for i in every]
    def onward(chips):
        return [
            (at(k, i), at(k + 2 * chips, i)) for k in range(segments - 2 * chips) for i in every
        ]

    beside = [
        pair
        for c in range(segments // 2) for i in range(groups - 1)
        for pair in (
            (at(2 * c + 1, i), at(2 * c, i + 1)), (at(2 * c, i + 1), at(2 * c + 1, i))
        )
    ]
    rounds = [
        [(i, i + 1) for i in range(first, groups - 1, 2)]
        + [(i + 1, i) for i in range(first, groups - 1, 2)]
        for first in range(2)
    ]

    left, right = in_hbm(left_env[0]), in_hbm(right_env[0])
    whole = (2, channels) + block
    own, other = pl.pallas_call(
        split_kernel,
        out_shape=[jax.ShapeDtypeStruct((2,) + block, BF16)] * 2,
        in_specs=anywhere(2),
        out_specs=vmem(2),
        scratch_shapes=[
            pltpu.VMEM((2,) + block, F32),
            pltpu.VMEM((2,) + block, BF16),
            pltpu.SemaphoreType.DMA((2,)),
        ],
        compiler_params=limit(4),
        cost_estimate=cost(0, size, 2 * MIB),
    )(in_hbm(gauge_offset[0]), in_hbm(state_blocks[0]))
    got = lax.ppermute(other, AXES, swap)
    cells, table = pl.pallas_call(
        table_kernel,
        out_shape=[
            jax.ShapeDtypeStruct((2,) + block, BF16),
            jax.ShapeDtypeStruct((4, channels), jnp.int32),
        ],
        in_specs=anywhere(3),
        out_specs=vmem(1) + smem(1),
        scratch_shapes=[
            pltpu.SMEM(charge.shape, jnp.int32),
            pltpu.SMEM(mpo_mask.shape, jnp.int32),
            pltpu.SMEM(block_dims.shape, jnp.int32),
            pltpu.SemaphoreType.DMA((3,)),
        ],
        compiler_params=limit(4),
        cost_estimate=cost(0, size, 2 * MIB),
    )(in_hbm(charge), in_hbm(mpo_mask), in_hbm(block_dims))

    pair = pl.pallas_call(
        pair_kernel,
        out_shape=jax.ShapeDtypeStruct(block, BF16),
        in_specs=vmem(2) + anywhere(1),
        out_specs=vmem(1)[0],
        compiler_params=limit(4),
        cost_estimate=cost(1, size, MIB),
    )(own, got, cells)
    backs = [lax.ppermute(pair, AXES, onward(chips)) for chips in range(1, segments // 2)]
    left_sorted, right_sorted = pl.pallas_call(
        sort_kernel,
        out_shape=[jax.ShapeDtypeStruct(whole, BF16)] * 2,
        in_specs=smem(1) + anywhere(2),
        out_specs=vmem(2),
        scratch_shapes=[pltpu.SemaphoreType.DMA((2, 2, channels))],
        compiler_params=limit(4),
        cost_estimate=cost(0, size, 16 * MIB),
    )(table, left, right)
    x_pair = pl.pallas_call(
        state_kernel,
        out_shape=jax.ShapeDtypeStruct((2,) + block, BF16),
        in_specs=vmem(6) + anywhere(1),
        out_specs=vmem(1)[0],
        scratch_shapes=[pltpu.VMEM((2, 2) + block, BF16)],
        compiler_params=limit(6),
        cost_estimate=cost(8, size, 2 * MIB),
    )(cells, own, got, *backs, right_sorted)
    x_swapped = lax.ppermute(x_pair, AXES, swap)
    side_beside = lax.ppermute(x_pair, AXES, beside)
    acc, env, x_here, crossing = pl.pallas_call(
        own_kernel,
        out_shape=[
            jax.ShapeDtypeStruct((2,) + block, F32),
            pltpu.HBM((1, 2, channels) + block, BF16),
            jax.ShapeDtypeStruct((2,) + block, BF16),
            jax.ShapeDtypeStruct((2, QUARTER) + block, BF16),
        ],
        in_specs=vmem(4) + anywhere(1),
        out_specs=vmem(1) + anywhere(1) + vmem(2),
        scratch_shapes=[
            pltpu.VMEM((2, size, channels * size), BF16),
            pltpu.VMEM((2, channels - QUARTER) + block, BF16),
            pltpu.SMEM((4, channels), jnp.int32),
            pltpu.SemaphoreType.DMA((1,)),
            pltpu.SemaphoreType.DMA((2, channels - QUARTER)),
        ],
        compiler_params=limit(12),
        cost_estimate=cost(96, size, 12 * MIB),
    )(x_pair, x_swapped, left_sorted, right_sorted, table)

    relayed = pl.pallas_call(
        relay_kernel,
        out_shape=jax.ShapeDtypeStruct(block, BF16),
        in_specs=vmem(1) + anywhere(1),
        out_specs=vmem(1)[0],
        compiler_params=limit(2),
        cost_estimate=cost(0, size, MIB),
    )(side_beside, acc)
    side_swapped = lax.ppermute(relayed, AXES, swap)
    to_first, to_second, sums, x_side = pl.pallas_call(
        image_kernel,
        out_shape=[
            jax.ShapeDtypeStruct((QUARTER + 1,) + block, BF16),
            jax.ShapeDtypeStruct((QUARTER + 1,) + block, BF16),
            pltpu.VMEM((groups, 128), F32),
            jax.ShapeDtypeStruct((2,) + block, BF16),
        ],
        in_specs=vmem(8),
        out_specs=vmem(4),
        scratch_shapes=[pltpu.VMEM((2, size, QUARTER * size), BF16)],
        compiler_params=limit(10),
        cost_estimate=cost(16, size, 4 * MIB),
    )(cells, x_here, side_beside, side_swapped, left_sorted, right_sorted, acc, crossing)
    from_first = lax.ppermute(to_first, "sec", rounds[0])
    from_second = lax.ppermute(to_second, "sec", rounds[1])
    image, sums_here = pl.pallas_call(
        apart_kernel,
        out_shape=[
            jax.ShapeDtypeStruct((2,) + block, F32),
            pltpu.VMEM((groups, 128), F32),
        ],
        in_specs=vmem(6),
        out_specs=vmem(2),
        scratch_shapes=[pltpu.VMEM((2, size, channels * size), BF16)],
        compiler_params=limit(10),
        cost_estimate=cost(48, size, 4 * MIB),
    )(sums, x_here, to_first, to_second, left_sorted, right_sorted)
    sums = lax.all_to_all(sums_here, "sec", 0, 0)

    total_cells = float(groups * 2 * size * size)
    krylov, env, rayleigh = pl.pallas_call(
        functools.partial(krylov_kernel, total_cells),
        out_shape=[
            jax.ShapeDtypeStruct((1, 2) + block, BF16),
            jax.ShapeDtypeStruct((1, 2, channels) + block, BF16),
            jax.ShapeDtypeStruct((1,), F32),
        ],
        in_specs=vmem(11) + anywhere(1),
        out_specs=vmem(1) + anywhere(1) + smem(1),
        scratch_shapes=[
            pltpu.VMEM((2, size, QUARTER * size), BF16),
            pltpu.SemaphoreType.DMA((2, QUARTER)),
        ],
        input_output_aliases={11: 1},
        compiler_params=limit(8),
        cost_estimate=cost(16, size, 4 * MIB),
    )(cells, sums, sums_here, image, acc, x_side, from_first, from_second, left_sorted,
      right_sorted, table, env)
    return krylov, env, rayleigh


def solution(mesh):
    return jax.shard_map(
        local,
        mesh=mesh,
        in_specs=(
            P("seg", "sec", None, None),
            P("seg", "sec", None, None),
            P("seg", "sec", None, None, None),
            P("seg", "sec", None, None, None),
            P("sec", None),
            P(),
            P("sec"),
        ),
        out_specs=(P("seg", "sec", None, None), P("seg", "sec", None, None, None), P("seg")),
        check_vma=False,
    )
```

```python
import functools

import jax
import jax.numpy as jnp
from jax import lax
from jax.experimental import pallas as pl
from jax.experimental.pallas import tpu as pltpu
from jax.sharding import PartitionSpec as P

F32 = jnp.float32
BF16 = jnp.bfloat16
AXES = ("seg", "sec")
QUARTER = 4
MIB = 1 << 20


def dot(first, second):
    return lax.dot_general(
        first, second, (((1,), (0,)), ((), ())), preferred_element_type=F32
    )


def vmem(count):
    return [pl.BlockSpec(memory_space=pltpu.VMEM)] * count


def smem(count):
    return [pl.BlockSpec(memory_space=pltpu.SMEM)] * count


def anywhere(count):
    return [pl.BlockSpec(memory_space=pl.ANY)] * count


def cost(products, size, bytes_accessed):
    return pl.CostEstimate(
        flops=2 * products * size**3, bytes_accessed=bytes_accessed, transcendentals=0
    )


def place():
    return lax.axis_index("seg") % 2


def odd_place():
    return lax.axis_index("sec") % 2 == 1


def limit(mebibytes):
    return pltpu.CompilerParams(vmem_limit_bytes=mebibytes * MIB)


def live(dim, size):
    rows = lax.broadcasted_iota(jnp.int32, (size, size), 0) < dim
    columns = lax.broadcasted_iota(jnp.int32, (size, size), 1) < dim
    return rows & columns


def in_hbm(array):
    return pltpu.with_memory_space_constraint(array, pltpu.HBM)


def split_kernel(gauge, state, own, other, gauge_here, state_here, sems):
    core = place()
    arrivals = [
        pltpu.make_async_copy(gauge, gauge_here, sems.at[0]),
        pltpu.make_async_copy(state, state_here, sems.at[1]),
    ]
    for copy in arrivals:
        copy.start()
    for copy in arrivals:
        copy.wait()
    own[0] = gauge_here[core].astype(BF16)
    own[1] = state_here[core]
    other[0] = gauge_here[1 - core].astype(BF16)
    other[1] = state_here[1 - core]


def table_kernel(charge_far, mask_far, dims_far, cells, table, charge, mask, dims, sems):
    channels, size = charge.shape[0], cells.shape[1]
    arrivals = [
        pltpu.make_async_copy(charge_far, charge, sems.at[0]),
        pltpu.make_async_copy(mask_far, mask, sems.at[1]),
        pltpu.make_async_copy(dims_far, dims, sems.at[2]),
    ]
    for copy in arrivals:
        copy.start()
    for copy in arrivals:
        copy.wait()
    ups, downs, rest = jnp.int32(0), jnp.int32(0), jnp.int32(0)
    for w in range(channels):
        up, down = charge[w] == 1, charge[w] == -1
        middle = QUARTER + rest
        table[0, jnp.where(up, ups, jnp.where(down, channels - QUARTER + downs, middle))] = w
        table[1, jnp.where(down, downs, jnp.where(up, channels - QUARTER + ups, middle))] = w
        ups = ups + up.astype(jnp.int32)
        downs = downs + down.astype(jnp.int32)
        rest = rest + jnp.where(up | down, 0, 1)
    for s in range(2):
        for j in range(channels):
            table[2 + s, j] = mask[s, table[s, j]]
        cells[s] = jnp.where(live(dims[s], size), 1.0, 0.0).astype(BF16)


def sort_kernel(table, left, right, left_sorted, right_sorted, sems):
    channels = left.shape[1]

    def copy(side, s, j):
        source, target = ((left, left_sorted), (right, right_sorted))[side]
        return pltpu.make_async_copy(
            source.at[s, table[s, j]], target.at[s, j], sems.at[side, s, j]
        )

    every = [(side, s, j) for side in range(2) for s in range(2) for j in range(channels)]
    for where in every:
        copy(*where).start()
    for where in every:
        copy(*where).wait()
    for s in range(2):
        for j in range(channels):
            @pl.when(table[2 + s, j] == 0)
            def _():
                right_sorted[s, j] = jnp.zeros(right_sorted.shape[2:], right_sorted.dtype)


def relay_kernel(pair, after, out):
    out[...] = pair[0]


def joined(later, earlier):
    return later.astype(F32) + earlier.astype(F32) + dot(later, earlier)


def pair_kernel(own, got, after, out):
    core = place()

    @pl.when(core == 0)
    def _():
        out[...] = joined(got[0], own[0]).astype(BF16)

    @pl.when(core == 1)
    def _():
        out[...] = joined(own[0], got[0]).astype(BF16)


def state_kernel(cells, own, got, one_back, two_back, three_back, *refs):
    x_pair, pair = refs[-2:]
    core = place()
    size = x_pair.shape[1]
    pair[core] = own[...]
    pair[1 - core] = got[...]
    field = jnp.concatenate([pair[0, 1], pair[1, 1]], axis=1)
    wide = field.astype(F32)
    wide = wide + dot(three_back[...], field)
    wide = wide + dot(two_back[...], wide.astype(BF16))
    wide = wide + dot(one_back[...], wide.astype(BF16))
    wide = wide + dot(pair[0, 0], wide.astype(BF16))
    earlier, later = wide[:, :size], wide[:, size:]
    later = later + dot(pair[1, 0], later.astype(BF16))
    alive = cells[core] != 0
    first = jnp.where(alive, earlier, 0.0).astype(BF16)
    second = jnp.where(alive, later, 0.0).astype(BF16)
    x_pair[core] = first
    x_pair[1 - core] = second


def spread(parts, s, blocks, field, first, last):
    size = field.shape[0]
    rows = blocks[s, first:last].reshape((last - first) * size, size)
    result = dot(rows, field).astype(BF16)
    for j in range(first, last):
        at = (j - first) * size
        parts[s, :, j * size : (j + 1) * size] = result[at : at + size]


def folded(parts, s, blocks, first, last):
    size = blocks.shape[-1]
    rows = blocks[s, first:last].reshape((last - first) * size, size)
    return dot(parts[s, :, first * size : last * size], rows)


def own_kernel(x_pair, x_swapped, left, table_far, env, x_here, crossing, parts, blocks, table,
               table_sem, out_sems):
    core = place()
    channels, size = left.shape[1], left.shape[2]
    cross = channels - QUARTER
    fetch = pltpu.make_async_copy(table_far, table, table_sem.at[0])
    fetch.start()
    x_here[core] = x_pair[0]
    x_here[1 - core] = x_swapped[1]

    def send(s, j):
        target = 1 - s if j < QUARTER else s
        return pltpu.make_async_copy(
            blocks.at[s, j], env.at[0, target, table[s, j]], out_sems.at[s, j]
        )

    for s in range(2):
        field = x_here[s]
        turned = field.T
        spread(parts, s, left, field, 0, channels)
        result = dot(turned, parts[s]).astype(BF16)
        for j in range(cross):
            blocks[s, j] = result[:, j * size : (j + 1) * size]
        for j in range(cross, channels):
            crossing[s, j - cross] = result[:, j * size : (j + 1) * size]
        if s == 0:
            fetch.wait()
        for j in range(cross):
            send(s, j).start()
    for s in range(2):
        for j in range(cross):
            send(s, j).wait()


def inner_kernel(x_here, left, right, parts, after, acc, side_parts):
    channels, size = left.shape[1], left.shape[2]
    cross = channels - QUARTER
    for s in range(2):
        rows = left[s, cross:channels].reshape(QUARTER * size, size)
        result = dot(rows, x_here[1 - s]).astype(BF16)
        for j in range(QUARTER):
            side_parts[s, :, j * size : (j + 1) * size] = result[j * size : (j + 1) * size]
        rows = right[s, cross:channels].reshape(QUARTER * size, size)
        acc[s] = folded(parts, s, right, QUARTER, cross) + dot(side_parts[s], rows)


def image_kernel(cells, x_here, side_beside, side_swapped, left, right, acc, crossing, to_first,
                 to_second, sums, x_side, parts):
    core = place()
    x_side[core] = side_beside[1]
    x_side[1 - core] = side_swapped[...]
    total = []
    for s in range(2):
        spread(parts, s, left, x_side[s], 0, QUARTER)
        image = acc[s] + folded(parts, s, right, 0, QUARTER)
        image = jnp.where(cells[s] != 0, image, 0.0).astype(BF16)
        total.append(image)
    odd = odd_place()
    for is_odd in range(2):
        @pl.when(odd == (is_odd == 1))
        def _():
            for s in range(2):
                message = (to_first, to_second)[s ^ is_odd ^ 1]
                message[:QUARTER] = crossing[s]
                message[QUARTER] = total[s]

    def whole(values):
        return jnp.sum(jnp.sum(values, axis=0, keepdims=True), axis=1, keepdims=True)

    x_wide = [x_here[s].astype(F32) for s in range(2)]
    v_wide = [total[s].astype(F32) for s in range(2)]
    norm = whole(x_wide[0] * x_wide[0] + x_wide[1] * x_wide[1])
    correlation = whole(x_wide[0] * v_wide[0] + x_wide[1] * v_wide[1])
    ratio = jnp.where(norm > 0.0, correlation / jnp.where(norm > 0.0, norm, 1.0), 0.0)
    apart = [v_wide[s] - ratio * x_wide[s] for s in range(2)]
    spread_of = whole(apart[0] * apart[0] + apart[1] * apart[1])
    lane = lax.broadcasted_iota(jnp.int32, sums.shape, 1)
    row = jnp.where(lane == 0, norm, jnp.where(lane == 1, correlation, 0.0))
    row = jnp.where(lane == 2, ratio, jnp.where(lane == 3, spread_of, row))
    sums[...] = row


def apart_kernel(sums, x_here, to_first, to_second, left, right, image, sums_out, parts):
    odd = odd_place()
    first, second = to_first[QUARTER], to_second[QUARTER]
    here = [jnp.where(odd, first, second), jnp.where(odd, second, first)]
    channels = left.shape[1]
    cross = channels - QUARTER
    ratio = sums[0:1, 2:3]

    def apart(v, x):
        return (v.astype(F32) - ratio * x.astype(F32)).astype(BF16)

    inner = [apart(here[s], x_here[s]) for s in range(2)]
    for s in range(2):
        spread(parts, s, left, inner[s], QUARTER, cross)
        spread(parts, s, left, inner[1 - s], cross, channels)
        image[s] = folded(parts, s, right, QUARTER, channels)
    sums_out[...] = sums[...]


def krylov_kernel(total_cells, cells, sums, sums_here, image, acc, x_side, from_first,
                  from_second, left, right, table, env_in, krylov, env, rayleigh, parts,
                  out_sems):
    odd = odd_place()
    place_of = [[table[s : s + 1, j : j + 1][0, 0] for j in range(QUARTER)] for s in range(2)]

    def send(is_odd, s, j):
        source = (from_first, from_second)[s ^ is_odd ^ 1]
        return pltpu.make_async_copy(
            source.at[j], env.at[0, s, place_of[s][j]], out_sems.at[s, j]
        )

    for is_odd in range(2):
        @pl.when(odd == (is_odd == 1))
        def _():
            for s in range(2):
                for j in range(QUARTER):
                    send(is_odd, s, j).start()
    column = [jnp.sum(sums[:, i : i + 1], axis=0, keepdims=True) for i in range(2)]
    ratio = column[1] / column[0]
    apart = ratio - sums[:, 2:3]
    spread_of = jnp.sum(sums[:, 3:4] + apart * apart * sums[:, 0:1], axis=0, keepdims=True)
    inverse = 1.0 / jnp.sqrt(spread_of * (1.0 / total_cells) + 1e-06)
    rayleigh[0] = ratio[0, 0]
    missing = ratio - sums_here[0:1, 2:3]
    first, second = from_first[QUARTER], from_second[QUARTER]
    arrived = [jnp.where(odd, first, second), jnp.where(odd, second, first)]
    for s in range(2):
        outer = (arrived[s].astype(F32) - ratio * x_side[s].astype(F32)).astype(BF16)
        spread(parts, s, left, outer, 0, QUARTER)
        whole = image[s] - missing * acc[s] + folded(parts, s, right, 0, QUARTER)
        krylov[0, s] = jnp.where(cells[s] != 0, whole * inverse, 0.0).astype(BF16)
    for is_odd in range(2):
        @pl.when(odd == (is_odd == 1))
        def _():
            for s in range(2):
                for j in range(QUARTER):
                    send(is_odd, s, j).wait()


def local(state_blocks, gauge_offset, left_env, right_env, mpo_mask, charge, block_dims):
    size = state_blocks.shape[-1]
    channels = left_env.shape[2]
    segments = lax.axis_size("seg")
    groups = lax.axis_size("sec")
    block = (size, size)

    def at(segment, group):
        return segment * groups + group

    every = range(groups)
    swap = [(at(k, i), at(k ^ 1, i)) for k in range(segments) for i in every]
    def onward(chips):
        return [
            (at(k, i), at(k + 2 * chips, i)) for k in range(segments - 2 * chips) for i in every
        ]

    beside = [
        pair
        for c in range(segments // 2) for i in range(groups - 1)
        for pair in (
            (at(2 * c + 1, i), at(2 * c, i + 1)), (at(2 * c, i + 1), at(2 * c + 1, i))
        )
    ]
    rounds = [
        [(i, i + 1) for i in range(first, groups - 1, 2)]
        + [(i + 1, i) for i in range(first, groups - 1, 2)]
        for first in range(2)
    ]

    left, right = in_hbm(left_env[0]), in_hbm(right_env[0])
    whole = (2, channels) + block
    own, other = pl.pallas_call(
        split_kernel,
        out_shape=[jax.ShapeDtypeStruct((2,) + block, BF16)] * 2,
        in_specs=anywhere(2),
        out_specs=vmem(2),
        scratch_shapes=[
            pltpu.VMEM((2,) + block, F32),
            pltpu.VMEM((2,) + block, BF16),
            pltpu.SemaphoreType.DMA((2,)),
        ],
        compiler_params=limit(4),
        cost_estimate=cost(0, size, 2 * MIB),
    )(in_hbm(gauge_offset[0]), in_hbm(state_blocks[0]))
    got = lax.ppermute(other, AXES, swap)
    cells, table = pl.pallas_call(
        table_kernel,
        out_shape=[
            jax.ShapeDtypeStruct((2,) + block, BF16),
            jax.ShapeDtypeStruct((4, channels), jnp.int32),
        ],
        in_specs=anywhere(3),
        out_specs=vmem(1) + smem(1),
        scratch_shapes=[
            pltpu.SMEM(charge.shape, jnp.int32),
            pltpu.SMEM(mpo_mask.shape, jnp.int32),
            pltpu.SMEM(block_dims.shape, jnp.int32),
            pltpu.SemaphoreType.DMA((3,)),
        ],
        compiler_params=limit(4),
        cost_estimate=cost(0, size, 2 * MIB),
    )(in_hbm(charge), in_hbm(mpo_mask), in_hbm(block_dims))

    pair = pl.pallas_call(
        pair_kernel,
        out_shape=jax.ShapeDtypeStruct(block, BF16),
        in_specs=vmem(2) + anywhere(1),
        out_specs=vmem(1)[0],
        compiler_params=limit(4),
        cost_estimate=cost(1, size, MIB),
    )(own, got, cells)
    backs = [lax.ppermute(pair, AXES, onward(chips)) for chips in range(1, segments // 2)]
    left_sorted, right_sorted = pl.pallas_call(
        sort_kernel,
        out_shape=[jax.ShapeDtypeStruct(whole, BF16)] * 2,
        in_specs=smem(1) + anywhere(2),
        out_specs=vmem(2),
        scratch_shapes=[pltpu.SemaphoreType.DMA((2, 2, channels))],
        compiler_params=limit(4),
        cost_estimate=cost(0, size, 16 * MIB),
    )(table, left, right)
    x_pair = pl.pallas_call(
        state_kernel,
        out_shape=jax.ShapeDtypeStruct((2,) + block, BF16),
        in_specs=vmem(6) + anywhere(1),
        out_specs=vmem(1)[0],
        scratch_shapes=[pltpu.VMEM((2, 2) + block, BF16)],
        compiler_params=limit(6),
        cost_estimate=cost(8, size, 2 * MIB),
    )(cells, own, got, *backs, right_sorted)
    x_swapped = lax.ppermute(x_pair, AXES, swap)
    side_beside = lax.ppermute(x_pair, AXES, beside)
    env, x_here, crossing, parts = pl.pallas_call(
        own_kernel,
        out_shape=[
            pltpu.HBM((1, 2, channels) + block, BF16),
            jax.ShapeDtypeStruct((2,) + block, BF16),
            jax.ShapeDtypeStruct((2, QUARTER) + block, BF16),
            jax.ShapeDtypeStruct((2, size, channels * size), BF16),
        ],
        in_specs=vmem(3) + anywhere(1),
        out_specs=anywhere(1) + vmem(3),
        scratch_shapes=[
            pltpu.VMEM((2, channels - QUARTER) + block, BF16),
            pltpu.SMEM((4, channels), jnp.int32),
            pltpu.SemaphoreType.DMA((1,)),
            pltpu.SemaphoreType.DMA((2, channels - QUARTER)),
        ],
        compiler_params=limit(12),
        cost_estimate=cost(72, size, 12 * MIB),
    )(x_pair, x_swapped, left_sorted, table)

    relayed = pl.pallas_call(
        relay_kernel,
        out_shape=jax.ShapeDtypeStruct(block, BF16),
        in_specs=vmem(1) + anywhere(1),
        out_specs=vmem(1)[0],
        compiler_params=limit(2),
        cost_estimate=cost(0, size, MIB),
    )(side_beside, x_here)
    side_swapped = lax.ppermute(relayed, AXES, swap)
    acc = pl.pallas_call(
        inner_kernel,
        out_shape=jax.ShapeDtypeStruct((2,) + block, F32),
        in_specs=vmem(4) + anywhere(1),
        out_specs=vmem(1)[0],
        scratch_shapes=[pltpu.VMEM((2, size, QUARTER * size), BF16)],
        compiler_params=limit(10),
        cost_estimate=cost(32, size, 4 * MIB),
    )(x_here, left_sorted, right_sorted, parts, relayed)
    to_first, to_second, sums, x_side = pl.pallas_call(
        image_kernel,
        out_shape=[
            jax.ShapeDtypeStruct((QUARTER + 1,) + block, BF16),
            jax.ShapeDtypeStruct((QUARTER + 1,) + block, BF16),
            pltpu.VMEM((groups, 128), F32),
            jax.ShapeDtypeStruct((2,) + block, BF16),
        ],
        in_specs=vmem(8),
        out_specs=vmem(4),
        scratch_shapes=[pltpu.VMEM((2, size, QUARTER * size), BF16)],
        compiler_params=limit(10),
        cost_estimate=cost(16, size, 4 * MIB),
    )(cells, x_here, side_beside, side_swapped, left_sorted, right_sorted, acc, crossing)
    from_first = lax.ppermute(to_first, "sec", rounds[0])
    from_second = lax.ppermute(to_second, "sec", rounds[1])
    image, sums_here = pl.pallas_call(
        apart_kernel,
        out_shape=[
            jax.ShapeDtypeStruct((2,) + block, F32),
            pltpu.VMEM((groups, 128), F32),
        ],
        in_specs=vmem(6),
        out_specs=vmem(2),
        scratch_shapes=[pltpu.VMEM((2, size, channels * size), BF16)],
        compiler_params=limit(10),
        cost_estimate=cost(48, size, 4 * MIB),
    )(sums, x_here, to_first, to_second, left_sorted, right_sorted)
    sums = lax.all_to_all(sums_here, "sec", 0, 0)

    total_cells = float(groups * 2 * size * size)
    krylov, env, rayleigh = pl.pallas_call(
        functools.partial(krylov_kernel, total_cells),
        out_shape=[
            jax.ShapeDtypeStruct((1, 2) + block, BF16),
            jax.ShapeDtypeStruct((1, 2, channels) + block, BF16),
            jax.ShapeDtypeStruct((1,), F32),
        ],
        in_specs=vmem(11) + anywhere(1),
        out_specs=vmem(1) + anywhere(1) + smem(1),
        scratch_shapes=[
            pltpu.VMEM((2, size, QUARTER * size), BF16),
            pltpu.SemaphoreType.DMA((2, QUARTER)),
        ],
        input_output_aliases={11: 1},
        compiler_params=limit(8),
        cost_estimate=cost(16, size, 4 * MIB),
    )(cells, sums, sums_here, image, acc, x_side, from_first, from_second, left_sorted,
      right_sorted, table, env)
    return krylov, env, rayleigh


def solution(mesh):
    return jax.shard_map(
        local,
        mesh=mesh,
        in_specs=(
            P("seg", "sec", None, None),
            P("seg", "sec", None, None),
            P("seg", "sec", None, None, None),
            P("seg", "sec", None, None, None),
            P("sec", None),
            P(),
            P("sec"),
        ),
        out_specs=(P("seg", "sec", None, None), P("seg", "sec", None, None, None), P("seg")),
        check_vma=False,
    )
```
